128 devices in a mesh: gz: 8 (over x, core), gy: 16 (over y, z).
Axes of the slice: x: 4, y: 4, z: 4, core: 2. Of those that a mesh axis runs over, the one named last changes fastest.
Arguments:
- source_volume: float32 [512, 1024, 512], P('gz', 'gy'), may hold values from -6 to 6
- target_volume: float32 [512, 1024, 512], P('gz', 'gy'), may hold values from -6 to 6
- live_count: int32 [8, 16], P('gz', 'gy'), may hold values from 0 to 8, as said below
- subset_start: int32 [8, 16, 8], P('gz', 'gy'), may hold values from 0 to 448
- patch_start: int32 [8, 16, 8], P('gz', 'gy'), may hold values from 0 to 448
- patch_shift: int32 [8, 16, 2, 8], P('gz', 'gy'), may hold values from -32 to 32
Outputs:
- correlation_window: float32 [8, 16, 8, 512], P('gz', 'gy')
The draws below stay inside these ranges and needn't reach their ends.
Inputs may be any that keep to these rules, and one draw needn't show every extreme that they name: The live subsets of a device are its first live_count slots. The counts of the two devices of one gz index whose gy indices differ by 8 add to exactly 8.
All inputs are finite; a program needn't handle non-finite values.
Results may differ from the reference program's by a relative error of at most 0.0003.
Values sent between devices are 32-bit elements; how exact they have to be, the bound alone decides.
No kernel may reach another device: no remote copies, remote signals or barrier semaphores. Data moves between devices by JAX's collectives and lax.ppermute only.
A program may use at most 512 MiB of HBM per device.

```python
import jax
import jax.numpy as jnp
from jax import lax

SUB = 64
WIN = 8
SUB_DEV = 8
NX = 512
DMAX = 32
NZ = 512
NY = 1024
N_GZ = 8
N_GY = 16


def edge_values(key, top_value):
    key_one, key_two = jax.random.split(key)
    values = jax.random.randint(key_one, (N_GZ, N_GY, SUB_DEV), 0, top_value + 1)
    lowest_slot = jax.random.randint(key_two, (N_GZ, N_GY, 1), 0, SUB_DEV)
    highest_slot = (lowest_slot + 1) % SUB_DEV
    positions = jnp.arange(SUB_DEV)[None, None, :]
    values = jnp.where(positions == lowest_slot, 0, values)
    values = jnp.where(positions == highest_slot, top_value, values)
    return values.astype(jnp.int32)


def draw_subset_start(key, part):
    key = jax.random.fold_in(key, 21)
    return edge_values(key, NX - SUB)


def draw_patch_start(key, part):
    key = jax.random.fold_in(key, 22)
    return edge_values(key, NX - SUB)


def draw_patch_shift(key, part):
    key = jax.random.fold_in(key, 23)
    key_one, key_two = jax.random.split(key)
    values = jax.random.randint(key_one, (N_GZ, N_GY, 2, SUB_DEV), -DMAX, DMAX + 1)
    chosen_slot = jax.random.randint(key_two, (N_GZ, N_GY, 1, 1), 0, SUB_DEV)
    positions = jnp.arange(SUB_DEV)[None, None, None, :]
    forced = jnp.array([DMAX, -DMAX], dtype=jnp.int32).reshape(1, 1, 2, 1)
    return jnp.where(positions == chosen_slot, forced, values).astype(jnp.int32)


def draw_live_count(key, part):
    key = jax.random.fold_in(key, 24)
    key_one, key_two, key_three = jax.random.split(key, 3)
    half_y = N_GY // 2
    lower = jax.random.randint(key_one, (N_GZ, half_y), 0, SUB_DEV + 1)
    row_pick = jax.random.randint(key_two, (), 0, N_GZ)
    column_pick = jax.random.randint(key_three, (), 0, half_y)
    marked = (jnp.arange(N_GZ)[:, None] == row_pick) & (jnp.arange(half_y)[None, :] == column_pick)
    lower = jnp.where(marked, SUB_DEV, lower)
    return jnp.concatenate([lower, SUB_DEV - lower], axis=1).astype(jnp.int32)


def block_scale(rng, shape, cuts, least, high):
    level, own = 1.0, jax.random.fold_in(rng, 6)
    for position, parts in cuts:
        draws = jnp.exp(jax.random.uniform(jax.random.fold_in(own, position), (parts,), jnp.float32, least / len(cuts), high / len(cuts)))
        level = level * jnp.repeat(draws, shape[position] // parts).reshape([-1 if axis == position else 1 for axis in range(len(shape))])
    return level


def scatter_about(own_key, extent, width, reach, cuts=(), kind=jnp.bfloat16):
    loudness = block_scale(own_key, extent, cuts, -0.22, 0.18) if cuts else 1.0
    values = jax.random.normal(own_key, extent, jnp.float32) * width * loudness
    return jnp.minimum(jnp.maximum(values, -reach), reach).astype(kind)


def setup_inputs(seed: int = 0) -> dict:
    streams_of = jax.random.split(jax.random.key(seed), 7)
    source_volume = scatter_about(streams_of[0], (NZ, NY, NX), 1.0, 6.0, ((0, 8), (1, 16)), jnp.float32)
    target_volume = scatter_about(streams_of[1], (NZ, NY, NX), 1.0, 6.0, ((0, 8), (1, 16)), jnp.float32)
    live_count = draw_live_count(jax.random.fold_in(streams_of[6], 71), 0)
    subset_start = draw_subset_start(jax.random.fold_in(streams_of[6], 71), 0)
    patch_start = draw_patch_start(jax.random.fold_in(streams_of[6], 71), 0)
    patch_shift = draw_patch_shift(jax.random.fold_in(streams_of[6], 71), 0)
    return dict(source_volume=source_volume, target_volume=target_volume, live_count=live_count, subset_start=subset_start, patch_start=patch_start, patch_shift=patch_shift)


def standardize(block_data):
    centred = block_data - jnp.mean(block_data)
    return centred * lax.rsqrt(jnp.mean(centred * centred) + 1e-05)

def reference(source_volume, target_volume, live_count, subset_start, patch_start, patch_shift):
    padded = jnp.pad(target_volume, ((DMAX, DMAX), (DMAX, DMAX), (0, 0)))
    shape_all = (N_GZ, N_GY, SUB_DEV)
    grid_z = jnp.broadcast_to(jnp.arange(N_GZ, dtype=jnp.int32)[:, None, None], shape_all).reshape(-1)
    grid_y = jnp.broadcast_to(jnp.arange(N_GY, dtype=jnp.int32)[None, :, None], shape_all).reshape(-1)
    slot_grid = jnp.broadcast_to(jnp.arange(SUB_DEV, dtype=jnp.int32)[None, None, :], shape_all).reshape(-1)
    counts = jnp.broadcast_to(live_count[:, :, None], shape_all).reshape(-1)
    items = (grid_z, grid_y, slot_grid, counts, subset_start.reshape(-1), patch_start.reshape(-1), patch_shift[:, :, 0].reshape(-1), patch_shift[:, :, 1].reshape(-1))

    def single(item_data):
        block_z, block_y, slot_index, count_here, start_x, corner_x, shift_z, shift_y = item_data
        source_block = lax.dynamic_slice(source_volume, (block_z * SUB, block_y * SUB, start_x), (SUB, SUB, SUB))
        target_block = lax.dynamic_slice(padded, (block_z * SUB + DMAX + shift_z, block_y * SUB + DMAX + shift_y, corner_x), (SUB, SUB, SUB))
        spectrum = jnp.conj(jnp.fft.fftn(standardize(source_block))) * jnp.fft.fftn(standardize(target_block))
        full_map = jnp.real(jnp.fft.ifftn(spectrum)) / float(SUB) ** 1.5
        half_win = WIN // 2
        cropped = jnp.roll(full_map, (half_win, half_win, half_win), axis=(0, 1, 2))[:WIN, :WIN, :WIN].reshape(WIN ** 3)
        return jnp.where(slot_index < count_here, cropped, jnp.zeros_like(cropped)).astype(jnp.float32)
    return lax.map(single, items).reshape(N_GZ, N_GY, SUB_DEV, WIN ** 3)
```

```python
import functools

import jax
import jax.numpy as jnp
from jax import lax
from jax.experimental import pallas as pl
from jax.experimental.pallas import tpu as pltpu
from jax.sharding import PartitionSpec as P

SUB = 64
WIN = 8
DMAX = 32
LANES = 128
TILES = 32
PAD = 2
CHUNK = 2
f32, bf16 = jnp.float32, jnp.bfloat16


def split(value):
    high = value.astype(bf16)
    return high, (value - high.astype(f32)).astype(bf16)


def half_roll(value):
    return pltpu.roll(value, 64, 1)


def slot_copies(stage, refs, meta, slot, buf, swin, qwin, sem, act):
    src, own, before_z, after_z, before_y, after_y, corner_before, corner_after = refs
    start, corner, shift_z, shift_y = (meta[n, slot] for n in range(4))

    def copy(condition, source, target, n):
        @pl.when(condition)
        def _():
            act(pltpu.make_async_copy(source, target, sem.at[buf, n]))

    for tile in range(2):
        at = start // LANES + tile
        lanes = pl.ds(pl.multiple_of(jnp.minimum(at, 3) * LANES, LANES), LANES)
        used = (tile == 0) | (lax.rem(start, LANES) > LANES - SUB)
        copy(used, src.at[:, :, lanes], swin.at[buf, tile], 2 * tile)

        at = corner // LANES + tile
        lanes = pl.ds(pl.multiple_of(jnp.minimum(at, 3) * LANES, LANES), LANES)
        used = (tile == 0) | (lax.rem(corner, LANES) > LANES - SUB)
        window = qwin.at[buf, tile]
        copy(used, own.at[:, :, lanes], window.at[DMAX:DMAX + SUB, DMAX:DMAX + SUB], 2 * tile + 1)
        copy(used & (shift_z < 0), before_z.at[:, :, lanes], window.at[:DMAX, DMAX:DMAX + SUB], 4 + tile)
        copy(used & (shift_z > 0), after_z.at[:, :, lanes], window.at[DMAX + SUB:, DMAX:DMAX + SUB], 4 + tile)
        for n in range(len(before_y)):
            here = used & (at == stage - n)
            up, down = here & (shift_y > 0), here & (shift_y < 0)
            copy(down, before_y[n], window.at[DMAX:DMAX + SUB, :DMAX], 6 + tile)
            copy(up, after_y[n], window.at[DMAX:DMAX + SUB, DMAX + SUB:], 6 + tile)
            for z_side, rows, piece in ((shift_z < 0, slice(0, DMAX), corner_before[n]),
                                        (shift_z > 0, slice(DMAX + SUB, None), corner_after[n])):
                copy(down & z_side, piece.at[:, :DMAX], window.at[rows, :DMAX], 8 + tile)
                copy(up & z_side, piece.at[:, DMAX:], window.at[rows, DMAX + SUB:], 8 + tile)


def align(win, buf, z0, row0, shift, flat):
    lane = lax.broadcasted_iota(jnp.int32, (SUB, LANES), 1)
    keep = lane >= shift
    left = lane < 64
    even_roll = lax.rem(LANES - shift, LANES)
    odd_roll = lax.rem(LANES + 64 - shift, LANES)

    def step(i, total):
        def row(z):
            a = win[buf, 0, z0 + z, pl.ds(row0, SUB), :]
            b = win[buf, 1, z0 + z, pl.ds(row0, SUB), :]
            return jnp.where(keep, a, b)
        even = pltpu.roll(row(2 * i), even_roll, 1)
        odd = pltpu.roll(row(2 * i + 1), odd_roll, 1)
        tile = jnp.where(left, even, odd)
        flat[:, pl.ds(pl.multiple_of(i * LANES, LANES), LANES)] = tile
        return total + jnp.sum(tile.reshape(8, 8, LANES), axis=0)

    total = lax.fori_loop(0, TILES, step, jnp.zeros((8, LANES), f32), unroll=2)
    return jnp.sum(total, keepdims=True) / float(SUB ** 3)


def kernel(stage, chunks, meta, *rest):
    src, own, before_z, after_z = rest[:4]
    pieces = [rest[4 + n * chunks:4 + (n + 1) * chunks] for n in range(4)]
    previous, out, swin, qwin, flat_s, flat_q, s_hi, s_lo, q_hi, q_lo, acc_a, acc_b, order, sem = rest[4 + 4 * chunks:]
    refs = (src, own, before_z, after_z, *pieces)
    out[...] = previous[...]
    left = lax.broadcasted_iota(jnp.int32, (SUB, LANES), 1) < 64
    within = lax.broadcasted_iota(jnp.int32, (SUB, LANES), 1) % 64

    count = jnp.int32(0)
    for slot in range(meta.shape[1]):
        mine = (slot < meta[4, 0]) & ((meta[1, slot] + SUB - 1) // LANES == stage)

        @pl.when(mine)
        def _(count=count, slot=slot):
            order[count] = slot
        count = count + mine.astype(jnp.int32)

    def copies(n, act):
        slot_copies(stage, refs, meta, order[n], lax.rem(n, 2), swin, qwin, sem, act)

    @pl.when(count > 0)
    def _():
        copies(0, lambda copy: copy.start())

    def one_slot(n, carry):
        slot, buf = order[n], lax.rem(n, 2)

        @pl.when(n + 1 < count)
        def _():
            copies(n + 1, lambda copy: copy.start())

        copies(n, lambda copy: copy.wait())
        mean_s = align(swin, buf, 0, 0, lax.rem(meta[0, slot], LANES), flat_s)
        mean_q = align(qwin, buf, meta[2, slot] + DMAX, meta[3, slot] + DMAX, lax.rem(meta[1, slot], LANES), flat_q)

        def source_step(i, square):
            here = flat_s[:, pl.ds(pl.multiple_of(i * LANES, LANES), LANES)] - mean_s
            j = lax.rem(i + 1, TILES)
            following = flat_s[:, pl.ds(pl.multiple_of(j * LANES, LANES), LANES)] - mean_s
            crossed = jnp.where(left, half_roll(here), half_roll(following))
            at = pl.ds(pl.multiple_of((i + PAD) * LANES, LANES), LANES)
            s_hi[0, :, at], s_lo[0, :, at] = split(here)
            s_hi[1, :, at], s_lo[1, :, at] = split(crossed)
            return square + jnp.sum((here * here).reshape(8, 8, LANES), axis=0)

        square_s = lax.fori_loop(0, TILES, source_step, jnp.zeros((8, LANES), f32), unroll=2)
        edge = PAD * LANES
        for ref in (s_hi, s_lo):
            ref[:, :, :edge] = ref[:, :, TILES * LANES:TILES * LANES + edge]
            ref[:, :, TILES * LANES + edge:] = ref[:, :, edge:2 * edge]

        def build(chunk, side):
            square = jnp.zeros((8, LANES), f32)
            for k in range(CHUNK):
                at = pl.ds(pl.multiple_of((chunk * CHUNK + k) * LANES, LANES), LANES)
                tile = flat_q[:, at] - mean_q
                square = square + jnp.sum((tile * tile).reshape(8, 8, LANES), axis=0)
                tile = jnp.concatenate([tile[56:], tile[:56]], axis=0)
                other = half_roll(tile)
                for n in range(WIN):
                    tx = n - WIN // 2
                    if tx == 0:
                        moved = tile
                    else:
                        take = within < tx if tx > 0 else within >= 64 + tx
                        moved = pltpu.roll(jnp.where(take, other, tile), (-tx) % LANES, 1)
                    high, low = split(moved)
                    q_hi[side, n * SUB:(n + 1) * SUB, k * LANES:(k + 1) * LANES] = high
                    q_lo[side, n * SUB:(n + 1) * SUB, k * LANES:(k + 1) * LANES] = low
            return square

        def source_rows(ref, chunk, w):
            rows = []
            for n in range(WIN):
                tz = n - WIN // 2
                parity = tz % 2
                offset = -(tz + parity) // 2
                at = pl.ds(pl.multiple_of((chunk * CHUNK + PAD + offset) * LANES, LANES), CHUNK * LANES)
                rows.append(ref[parity, 16 * w:16 * w + 16, at])
            return rows

        def target_rows(ref, side, w):
            rows = []
            for n in range(WIN):
                for j in (w, (w + 1) % 4):
                    rows.append(ref[side, n * SUB + 16 * j:n * SUB + 16 * j + 16, :])
            return jnp.concatenate(rows, axis=0)

        dims = (((1,), (1,)), ((), ()))

        def multiply(chunk, side):
            lhs, rhs_hi, rhs_lo = [], [], []
            for w in range(4):
                lhs.append(jnp.concatenate(source_rows(s_hi, chunk, w) + source_rows(s_lo, chunk, w), axis=0))
                rhs_hi.append(target_rows(q_hi, side, w))
                rhs_lo.append(target_rows(q_lo, side, w))
            lhs = jnp.concatenate(lhs, axis=1)
            acc_a[...] += lax.dot_general(lhs, jnp.concatenate(rhs_hi, axis=1), dims, preferred_element_type=f32)
            acc_b[...] += lax.dot_general(lhs[:128], jnp.concatenate(rhs_lo, axis=1), dims, preferred_element_type=f32)

        acc_a[...] = jnp.zeros_like(acc_a)
        acc_b[...] = jnp.zeros_like(acc_b)
        steps = TILES // CHUNK
        square_q = build(0, 0)

        def pair(i, square):
            first = build(2 * i + 1, 1)
            multiply(2 * i, 0)
            second = build(lax.rem(2 * i + 2, steps), 0)
            multiply(2 * i + 1, 1)
            return square + first + jnp.where(2 * i + 2 < steps, second, 0.0)

        square_q = lax.fori_loop(0, steps // 2, pair, square_q)
        scale = lax.rsqrt(jnp.sum(square_s, keepdims=True) / float(SUB ** 3) + 1e-5)
        scale = scale * lax.rsqrt(jnp.sum(square_q, keepdims=True) / float(SUB ** 3) + 1e-5)
        scale = scale * (1.0 / float(SUB) ** 1.5)
        total = (acc_a[:128, :] + acc_a[128:, :] + acc_b[...]).reshape(WIN, 16, 256)
        row = lax.broadcasted_iota(jnp.int32, (16, 256), 0)
        column = lax.broadcasted_iota(jnp.int32, (16, 256), 1) % 32
        picked = []
        for n in range(WIN):
            picked.append(jnp.sum(jnp.where((column == row + n + 4)[None], total, 0.0), axis=1))
        picked = jnp.stack(picked, axis=1).reshape(WIN * WIN, 256)
        group = lax.broadcasted_iota(jnp.int32, (256, LANES), 0) // 32
        gather = (group == lax.broadcasted_iota(jnp.int32, (256, LANES), 1)).astype(f32)
        result = jnp.dot(picked, gather, precision=lax.Precision.HIGHEST, preferred_element_type=f32)
        out[pl.ds(slot, 1)] = (result * scale)[None]
        return carry

    lax.fori_loop(0, count, one_slot, 0)


def correlate(stage, meta, source, target, halo_z, halo_y, corners, previous):
    slots = meta.shape[1]
    first = max(stage - 1, 0)
    pieces = []
    for pair in (halo_y, corners):
        for side in range(2):
            pieces += [pair[n][side] for n in range(stage, first - 1, -1)]
    any_space = pl.BlockSpec(memory_space=pl.ANY)
    in_vmem = pl.BlockSpec(memory_space=pltpu.VMEM)
    return pl.pallas_call(
        functools.partial(kernel, stage, stage - first + 1),
        out_shape=jax.ShapeDtypeStruct((slots, WIN * WIN, LANES), f32),
        in_specs=[pl.BlockSpec(memory_space=pltpu.SMEM)] + [any_space] * (4 + len(pieces)) + [in_vmem],
        out_specs=in_vmem,
        scratch_shapes=[
            pltpu.VMEM((2, 2, SUB, SUB, LANES), f32),
            pltpu.VMEM((2, 2, SUB + 2 * DMAX, SUB + 2 * DMAX, LANES), f32),
            pltpu.VMEM((SUB, TILES * LANES), f32),
            pltpu.VMEM((SUB, TILES * LANES), f32),
            pltpu.VMEM((2, SUB, (TILES + 2 * PAD) * LANES), bf16),
            pltpu.VMEM((2, SUB, (TILES + 2 * PAD) * LANES), bf16),
            pltpu.VMEM((2, WIN * SUB, CHUNK * LANES), bf16),
            pltpu.VMEM((2, WIN * SUB, CHUNK * LANES), bf16),
            pltpu.VMEM((256, 256), f32),
            pltpu.VMEM((128, 256), f32),
            pltpu.SMEM((slots,), jnp.int32),
            pltpu.SemaphoreType.DMA((2, 10)),
        ],
        compiler_params=pltpu.CompilerParams(vmem_limit_bytes=58 * 1024 * 1024),
        cost_estimate=pl.CostEstimate(flops=2 * 2 * 3 * 512 * 2 ** 20, bytes_accessed=2 * 9 * 2 ** 20, transcendentals=0),
        name="correlate",
    )(meta, source, target, *halo_z, *pieces, previous)


def neighbours(axis, low, high):
    peers = lax.axis_size(axis)
    up = [(i, i + 1) for i in range(peers - 1)]
    return lax.ppermute(high, axis, up), lax.ppermute(low, axis, [(j, i) for i, j in up])


def per_device(source_volume, target_volume, live_count, subset_start, patch_start, patch_shift):
    slots = subset_start.shape[-1]
    meta = jnp.stack([
        subset_start[0, 0], patch_start[0, 0], patch_shift[0, 0, 0], patch_shift[0, 0, 1],
        jnp.broadcast_to(live_count[0, 0], (slots,)),
    ])
    stages = target_volume.shape[-1] // LANES
    halo_y = []
    for k in range(stages):
        part = target_volume[:, :, k * LANES:(k + 1) * LANES]
        halo_y.append(neighbours("gy", part[:, :DMAX], part[:, -DMAX:]))
        if k == 0:
            halo_z = neighbours("gz", target_volume[:DMAX], target_volume[-DMAX:])
    corners = []
    out = jnp.zeros((slots, WIN * WIN, LANES), f32)
    for k in range(stages):
        before, after = halo_y[k]
        low = jnp.concatenate([before[:DMAX], after[:DMAX]], axis=1)
        high = jnp.concatenate([before[-DMAX:], after[-DMAX:]], axis=1)
        corners.append(neighbours("gz", low, high))
        out = correlate(k, meta, source_volume, target_volume, halo_z, halo_y, corners, out)
    return out[:, :, :WIN].reshape(1, 1, slots, WIN ** 3)


def solution(mesh):
    return jax.shard_map(
        per_device,
        mesh=mesh,
        in_specs=(
            P("gz", "gy", None),
            P("gz", "gy", None),
            P("gz", "gy"),
            P("gz", "gy", None),
            P("gz", "gy", None),
            P("gz", "gy", None, None),
        ),
        out_specs=P("gz", "gy", None, None),
        check_vma=False,
    )
```

```python
import functools

import jax
import jax.numpy as jnp
from jax import lax
from jax.experimental import pallas as pl
from jax.experimental.pallas import tpu as pltpu
from jax.sharding import PartitionSpec as P

SUB = 64
WIN = 8
DMAX = 32
LANES = 128
TILES = 32
PAD = 2
CHUNK = 4
WIDTH = (TILES + 2 * PAD) * LANES
STEP_X = 4
PIECES = (2, 1, 1)
EARLY = 2
f32, bf16 = jnp.float32, jnp.bfloat16


def split(value):
    high = value.astype(bf16)
    return high, (value - high.astype(f32)).astype(bf16)


def half_roll(value):
    return pltpu.roll(value, 64, 1)


def lane_index(rows=SUB):
    return lax.broadcasted_iota(jnp.int32, (rows, LANES), 1)


def fold(tile):
    return jnp.sum(tile.reshape(8, 8, LANES), axis=0)


def turned(tile, other, shift):
    moved = jnp.where(lane_index() % 64 < shift, other, tile)
    return pltpu.roll(moved, LANES - shift, 1)


def tile_at(i):
    return pl.ds(pl.multiple_of(i * LANES, LANES), LANES)


def aligned(row, i, shift):
    even = pltpu.roll(row(2 * i), lax.rem(LANES - shift, LANES), 1)
    odd = pltpu.roll(row(2 * i + 1), lax.rem(LANES + 64 - shift, LANES), 1)
    return jnp.where(lane_index() < 64, even, odd)


def prepare_kernel(meta, first, second, high_ref, low_ref, scale_ref, flat):
    slot = pl.program_id(0)

    @pl.when(slot < meta[4, 0])
    def _():
        shift = lax.rem(meta[0, slot], LANES)
        keep = lane_index() >= shift

        def row(z):
            return jnp.where(keep, first[z], second[z])

        def gather(i, total):
            tile = aligned(row, i, shift)
            flat[:, tile_at(i)] = tile
            return total + fold(tile)

        total = lax.fori_loop(0, TILES, gather, jnp.zeros((8, LANES), f32), unroll=4)
        mean = jnp.sum(total, keepdims=True) / float(SUB ** 3)

        def cross(i, square):
            here = flat[:, tile_at(i)] - mean
            following = flat[:, tile_at(lax.rem(i + 1, TILES))] - mean
            left = lane_index() < 64
            here_half, following_half = half_roll(here), half_roll(following)
            crossed = jnp.where(left, here_half, following_half)
            crossed_half = jnp.where(left, following, here)
            forms = [here, crossed, turned(here, here_half, STEP_X), turned(crossed, crossed_half, STEP_X)]
            for n, form in enumerate(forms):
                high_ref[0, n, :, tile_at(i + PAD)], low_ref[0, n, :, tile_at(i + PAD)] = split(form)
            return square + fold(here * here)

        square = lax.fori_loop(0, TILES, cross, jnp.zeros((8, LANES), f32), unroll=4)
        edge = PAD * LANES
        for ref in (high_ref, low_ref):
            ref[:, :, :, :edge] = ref[:, :, :, TILES * LANES:TILES * LANES + edge]
            ref[:, :, :, TILES * LANES + edge:] = ref[:, :, :, edge:2 * edge]
        scale = lax.rsqrt(jnp.sum(square, keepdims=True) / float(SUB ** 3) + 1e-5)
        scale_ref[0] = jnp.broadcast_to(scale, (8, LANES))


def prepare(meta, source):
    slots = meta.shape[1]
    block = (SUB, SUB, LANES)
    spread = pl.BlockSpec((1, 4, SUB, WIDTH), lambda s, m: (s, 0, 0, 0))
    rows = jax.ShapeDtypeStruct((slots, 4, SUB, WIDTH), bf16)
    return pl.pallas_call(
        prepare_kernel,
        out_shape=[rows, rows, jax.ShapeDtypeStruct((slots, 8, LANES), f32)],
        grid_spec=pltpu.PrefetchScalarGridSpec(
            num_scalar_prefetch=1,
            grid=(slots,),
            in_specs=[
                pl.BlockSpec(block, lambda s, m: (0, 0, m[0, s] // LANES)),
                pl.BlockSpec(block, lambda s, m: (0, 0, jnp.minimum(m[0, s] // LANES + 1, 3))),
            ],
            out_specs=[spread, spread, pl.BlockSpec((1, 8, LANES), lambda s, m: (s, 0, 0))],
            scratch_shapes=[pltpu.VMEM((SUB, TILES * LANES), f32)],
        ),
        compiler_params=pltpu.CompilerParams(vmem_limit_bytes=40 * 1024 * 1024),
        cost_estimate=pl.CostEstimate(flops=1, bytes_accessed=1, transcendentals=0),
        name="prepare",
    )(meta, source, source)


def window_copies(parts, refs, meta, slot, buf, window, sem, act):
    own, before_z, after_z, before_y, after_y, corner_before, corner_after = refs
    corner, shift_z, shift_y = meta[1, slot], meta[2, slot], meta[3, slot]
    middle = slice(DMAX, DMAX + SUB)
    edges = slice(0, DMAX), slice(DMAX + SUB, SUB + 2 * DMAX)

    def copy(source, z_rows, y_rows, tile, n):
        act(pltpu.make_async_copy(source, window.at[buf, tile, z_rows, y_rows], sem.at[buf, n, tile]))

    for tile in range(2):
        at = corner // LANES + tile

        @pl.when((tile == 0) | (lax.rem(corner, LANES) > LANES - SUB))
        def _(tile=tile, at=at):
            lanes = tile_at(jnp.minimum(at, 3))
            copy(own.at[:, :, lanes], middle, middle, tile, 0)
            for side, halo in enumerate((before_z, after_z)):
                @pl.when(shift_z < 0 if side == 0 else shift_z > 0)
                def _(side=side, halo=halo):
                    copy(halo.at[:, :, lanes], edges[side], middle, tile, 1)

            for y_side in range(2):
                @pl.when(shift_y < 0 if y_side == 0 else shift_y > 0)
                def _(y_side=y_side):
                    for n, part in enumerate(parts):
                        base = sum(PIECES[:part])

                        @pl.when((at >= base) & (at < base + PIECES[part]))
                        def _(n=n, base=base):
                            here = tile_at(at - base)
                            copy((before_y, after_y)[y_side][n].at[:, :, here], middle, edges[y_side], tile, 2)
                            for z_side in range(2):
                                @pl.when(shift_z < 0 if z_side == 0 else shift_z > 0)
                                def _(z_side=z_side):
                                    piece = (corner_before, corner_after)[z_side][n]
                                    piece = piece.at[:, y_side * DMAX:(y_side + 1) * DMAX, here]
                                    copy(piece, edges[z_side], edges[y_side], tile, 3)


def kernel(call, parts, meta, scales, s_high, s_low, *rest):
    chunks = len(parts)
    own, before_z, after_z = rest[:3]
    pieces = [rest[3 + n * chunks:3 + (n + 1) * chunks] for n in range(4)]
    previous, out, window, flat, s_hi, s_lo, q_hi, q_lo, acc_a, acc_b, order, q_sem, s_sem = rest[3 + 4 * chunks:]
    refs = (own, before_z, after_z, *pieces)
    out[...] = previous[...]

    count, early = jnp.int32(0), jnp.int32(0)
    for slot in range(meta.shape[1]):
        stage = (meta[1, slot] + SUB - 1) // LANES
        live = slot < meta[4, 0]
        first = live & (stage < PIECES[0]) & (early < EARLY)
        early = early + first.astype(jnp.int32)
        mine = (first, live & (stage < 3) & jnp.logical_not(first), live & (stage == 3))[call]

        @pl.when(mine)
        def _(count=count, slot=slot):
            order[count] = slot
        count = count + mine.astype(jnp.int32)

    def windows(n, buf, act):
        window_copies(parts, refs, meta, order[n], buf, window, q_sem, act)

    def sources(n, buf, act):
        act(pltpu.make_async_copy(s_high.at[order[n]], s_hi.at[buf], s_sem.at[buf, 0]))
        act(pltpu.make_async_copy(s_low.at[order[n]], s_lo.at[buf], s_sem.at[buf, 1]))

    start, wait = (lambda copy: copy.start()), (lambda copy: copy.wait())

    def gather(n, buf):
        slot = order[n]
        shift = lax.rem(meta[1, slot], LANES)
        z0, y0 = meta[2, slot] + DMAX, meta[3, slot] + DMAX
        keep = lane_index() >= shift

        def row(z):
            rows = pl.ds(y0, SUB)
            return jnp.where(keep, window[buf, 0, z0 + z, rows, :], window[buf, 1, z0 + z, rows, :])

        def step(i):
            tile = aligned(row, i, shift)
            flat[buf, :, tile_at(i)] = tile
            return fold(tile)

        return step

    def average(total):
        return jnp.sum(total, keepdims=True) / float(SUB ** 3)

    zero = jnp.zeros((8, LANES), f32)
    steps = TILES // CHUNK
    dims = (((1,), (1,)), ((), ()))

    def source_rows(ref, buf, chunk, w):
        rows = []
        for a in range(2):
            for n in range(WIN):
                tz = n - WIN // 2
                parity = tz % 2
                offset = PAD - (tz + parity) // 2
                at = pl.ds(pl.multiple_of((chunk * CHUNK + offset) * LANES, LANES), CHUNK * LANES)
                rows.append(ref[buf, 2 * a + parity, 16 * w:16 * w + 16, at])
        return jnp.concatenate(rows, axis=0)

    def target_rows(ref, side, w):
        rows = []
        for n in range(STEP_X):
            for j in (w, (w + 1) % 4):
                rows.append(ref[side, n * SUB + 16 * j:n * SUB + 16 * j + 16, :])
        return rows

    def multiply(buf, chunk, side):
        lhs = jnp.concatenate([
            jnp.concatenate(target_rows(q_hi, side, w) + target_rows(q_lo, side, w), axis=0) for w in range(4)], axis=1)
        rhs_hi = jnp.concatenate([source_rows(s_hi, buf, chunk, w) for w in range(4)], axis=1)
        rhs_lo = jnp.concatenate([source_rows(s_lo, buf, chunk, w) for w in range(4)], axis=1)
        acc_a[...] += lax.dot_general(lhs, rhs_hi, dims, preferred_element_type=f32)
        acc_b[...] += lax.dot_general(lhs[:128], rhs_lo, dims, preferred_element_type=f32)

    def one_slot(n, buf, mean):
        slot = order[n]

        @pl.when(n + 2 < count)
        def _():
            windows(n + 2, buf, start)

        @pl.when(n + 1 < count)
        def _():
            sources(n + 1, 1 - buf, start)
            windows(n + 1, 1 - buf, wait)

        sources(n, buf, wait)
        gather_step = gather(jnp.minimum(n + 1, count - 1), 1 - buf)

        def build(chunk, side):
            square = zero
            for k in range(CHUNK):
                tile = flat[buf, :, tile_at(chunk * CHUNK + k)] - mean
                square = square + fold(tile * tile)
                tile = jnp.concatenate([tile[56:], tile[:56]], axis=0)
                other = half_roll(tile)
                for b in range(STEP_X):
                    moved = turned(tile, other, b) if b else tile
                    high, low = split(moved)
                    q_hi[side, b * SUB:(b + 1) * SUB, k * LANES:(k + 1) * LANES] = high
                    q_lo[side, b * SUB:(b + 1) * SUB, k * LANES:(k + 1) * LANES] = low
            return square

        acc_a[...] = jnp.zeros_like(acc_a)
        acc_b[...] = jnp.zeros_like(acc_b)
        square = build(0, 0)

        def two_steps(i, carry):
            square, total = carry
            for side in range(2):
                chunk = 2 * i + side
                more = build(lax.rem(chunk + 1, steps), 1 - side)
                square = square + (more if side == 0 else jnp.where(chunk + 1 < steps, more, 0.0))
                multiply(buf, chunk, side)
                for k in range(CHUNK):
                    total = total + gather_step(chunk * CHUNK + k)
            return square, total

        square, total = lax.fori_loop(0, steps // 2, two_steps, (square, zero), unroll=4)
        scale = scales[pl.ds(slot, 1)][0, :1, :1] * lax.rsqrt(average(square) + 1e-5) * (1.0 / float(SUB) ** 1.5)
        sums = (acc_a[:128, :] + acc_a[128:, :] + acc_b[...]).reshape(STEP_X, 32, 256)
        row = lax.broadcasted_iota(jnp.int32, (32, 256), 0)
        column = lax.broadcasted_iota(jnp.int32, (32, 256), 1) % 16
        picked = [jnp.sum(jnp.where((row == column + n + 4)[None], sums, 0.0), axis=1) for n in range(WIN)]
        picked = jnp.concatenate(picked, axis=0)
        group = lax.broadcasted_iota(jnp.int32, (256, LANES), 0) // 16
        chosen = (group == lax.broadcasted_iota(jnp.int32, (256, LANES), 1)).astype(f32)
        result = jnp.dot(picked, chosen, precision=lax.Precision.HIGHEST, preferred_element_type=f32)
        out[pl.ds(slot, 1)] = (result * scale)[None]
        return average(total)

    @pl.when(count > 0)
    def _():
        windows(0, 0, start)
        sources(0, 0, start)

        @pl.when(count > 1)
        def _():
            windows(1, 1, start)

        windows(0, 0, wait)
        first = gather(0, 0)
        total = lax.fori_loop(0, TILES, lambda i, total: total + first(i), zero, unroll=4)

        def two_slots(m, mean):
            mean = one_slot(2 * m, 0, mean)
            return lax.cond(2 * m + 1 < count, lambda: one_slot(2 * m + 1, 1, mean), lambda: mean)

        lax.fori_loop(0, (count + 1) // 2, two_slots, average(total))


def correlate(call, parts, meta, prepared, target, halo_z, halo_y, corners, previous):
    slots = meta.shape[1]
    s_high, s_low, scales = prepared
    pieces = []
    for pair in (halo_y, corners):
        for side in range(2):
            pieces += [pair[n][side] for n in parts]
    any_space = pl.BlockSpec(memory_space=pl.ANY)
    in_vmem = pl.BlockSpec(memory_space=pltpu.VMEM)
    reach = SUB + 2 * DMAX
    return pl.pallas_call(
        functools.partial(kernel, call, parts),
        out_shape=jax.ShapeDtypeStruct((slots, 4 * WIN, LANES), f32),
        in_specs=[pl.BlockSpec(memory_space=pltpu.SMEM), in_vmem] + [any_space] * (5 + len(pieces)) + [in_vmem],
        out_specs=in_vmem,
        scratch_shapes=[
            pltpu.VMEM((2, 2, reach, reach, LANES), f32),
            pltpu.VMEM((2, SUB, TILES * LANES), f32),
            pltpu.VMEM((2, 4, SUB, WIDTH), bf16),
            pltpu.VMEM((2, 4, SUB, WIDTH), bf16),
            pltpu.VMEM((2, STEP_X * SUB, CHUNK * LANES), bf16),
            pltpu.VMEM((2, STEP_X * SUB, CHUNK * LANES), bf16),
            pltpu.VMEM((256, 256), f32),
            pltpu.VMEM((128, 256), f32),
            pltpu.SMEM((slots,), jnp.int32),
            pltpu.SemaphoreType.DMA((2, 4, 2)),
            pltpu.SemaphoreType.DMA((2, 2)),
        ],
        compiler_params=pltpu.CompilerParams(vmem_limit_bytes=58 * 1024 * 1024),
        cost_estimate=pl.CostEstimate(flops=1, bytes_accessed=1, transcendentals=0),
        name="correlate",
    )(meta, scales, s_high, s_low, target, *halo_z, *pieces, previous)


def assemble(out):
    slots = out.shape[0]
    sums = out[:, :, :2 * WIN].reshape(slots, WIN, STEP_X, 2, WIN)
    return sums[:, :, :, ::-1].transpose(0, 4, 1, 3, 2).reshape(slots, WIN ** 3)


def neighbours(axis, low, high):
    peers = lax.axis_size(axis)
    up = [(i, i + 1) for i in range(peers - 1)]
    return lax.ppermute(high, axis, up), lax.ppermute(low, axis, [(j, i) for i, j in up])


def per_device(source_volume, target_volume, live_count, subset_start, patch_start, patch_shift):
    slots = subset_start.shape[-1]
    meta = jnp.stack([
        subset_start[0, 0], patch_start[0, 0], patch_shift[0, 0, 0], patch_shift[0, 0, 1],
        jnp.broadcast_to(live_count[0, 0], (slots,)),
    ])
    cuts, base = [], 0
    for width in PIECES:
        cuts.append(slice(base * LANES, (base + width) * LANES))
        base += width

    def edges(volume, cut):
        return volume[:, :DMAX, cut], volume[:, -DMAX:, cut]

    def send_corners(pair):
        before, after = pair
        low = jnp.concatenate([before[:DMAX], after[:DMAX]], axis=1)
        high = jnp.concatenate([before[-DMAX:], after[-DMAX:]], axis=1)
        return neighbours("gz", low, high)

    low, high, later = lax.optimization_barrier((*edges(target_volume, cuts[0]), target_volume))
    halo_y = [neighbours("gy", low, high)]
    halo_z = neighbours("gz", later[:DMAX], later[-DMAX:])
    prepared = prepare(meta, source_volume)
    low, high = edges(later, cuts[1])
    halo_y[0], prepared, low, high, low2, high2 = lax.optimization_barrier((halo_y[0], prepared, low, high, *edges(later, cuts[2])))
    halo_y.append(neighbours("gy", low, high))
    halo_z, before, after = lax.optimization_barrier((halo_z, *halo_y[0]))
    corners = [send_corners((before, after))]
    low2, high2, halo_y[1], halo_z = lax.optimization_barrier((low2, high2, halo_y[1], halo_z))
    halo_y.append(neighbours("gy", low2, high2))
    corners.append(send_corners(halo_y[1]))
    out = jnp.zeros((slots, 4 * WIN, LANES), f32)
    out = correlate(0, (0,), meta, prepared, target_volume, halo_z, halo_y, corners, out)
    halo_y[2], out = lax.optimization_barrier((halo_y[2], out))
    corners.append(send_corners(halo_y[2]))
    out = correlate(1, (0, 1), meta, prepared, target_volume, halo_z, halo_y, corners, out)
    out = correlate(2, (1, 2), meta, prepared, target_volume, halo_z, halo_y, corners, out)
    return assemble(out)[None, None]


def solution(mesh):
    return jax.shard_map(
        per_device,
        mesh=mesh,
        in_specs=(
            P("gz", "gy", None),
            P("gz", "gy", None),
            P("gz", "gy"),
            P("gz", "gy", None),
            P("gz", "gy", None),
            P("gz", "gy", None, None),
        ),
        out_specs=P("gz", "gy", None, None),
        check_vma=False,
    )
```

```python
import functools

import jax
import jax.numpy as jnp
from jax import lax
from jax.experimental import pallas as pl
from jax.experimental.pallas import tpu as pltpu
from jax.sharding import PartitionSpec as P

SUB = 64
WIN = 8
DMAX = 32
LANES = 128
TILES = 32
PAD = 2
CHUNK = 4
WIDTH = (TILES + 2 * PAD) * LANES
STEP_X = 4
PIECES = (3, 1)
EARLY = 8
f32, bf16 = jnp.float32, jnp.bfloat16


def split(value):
    high = value.astype(bf16)
    return high, (value - high.astype(f32)).astype(bf16)


def half_roll(value):
    return pltpu.roll(value, 64, 1)


def lane_index(rows=SUB):
    return lax.broadcasted_iota(jnp.int32, (rows, LANES), 1)


def fold(tile):
    return jnp.sum(tile.reshape(8, 8, LANES), axis=0)


def turned(tile, other, shift):
    moved = jnp.where(lane_index() % 64 < shift, other, tile)
    return pltpu.roll(moved, LANES - shift, 1)


def tile_at(i):
    return pl.ds(pl.multiple_of(i * LANES, LANES), LANES)


def aligned(row, i, shift):
    even = pltpu.roll(row(2 * i), lax.rem(LANES - shift, LANES), 1)
    odd = pltpu.roll(row(2 * i + 1), lax.rem(LANES + 64 - shift, LANES), 1)
    return jnp.where(lane_index() < 64, even, odd)


def prepare_kernel(meta, first, second, high_ref, low_ref, scale_ref, flat):
    slot = pl.program_id(0)

    @pl.when(slot < meta[4, 0])
    def _():
        shift = lax.rem(meta[0, slot], LANES)
        keep = lane_index() >= shift

        def row(z):
            return jnp.where(keep, first[z], second[z])

        def gather(i, total):
            tile = aligned(row, i, shift)
            flat[:, tile_at(i)] = tile
            return total + fold(tile)

        total = lax.fori_loop(0, TILES, gather, jnp.zeros((8, LANES), f32), unroll=4)
        mean = jnp.sum(total, keepdims=True) / float(SUB ** 3)

        def cross(i, square):
            here = flat[:, tile_at(i)] - mean
            following = flat[:, tile_at(lax.rem(i + 1, TILES))] - mean
            left = lane_index() < 64
            here_half, following_half = half_roll(here), half_roll(following)
            crossed = jnp.where(left, here_half, following_half)
            crossed_half = jnp.where(left, following, here)
            forms = [here, crossed, turned(here, here_half, STEP_X), turned(crossed, crossed_half, STEP_X)]
            for n, form in enumerate(forms):
                high_ref[0, n, :, tile_at(i + PAD)], low_ref[0, n, :, tile_at(i + PAD)] = split(form)
            return square + fold(here * here)

        square = lax.fori_loop(0, TILES, cross, jnp.zeros((8, LANES), f32), unroll=4)
        edge = PAD * LANES
        for ref in (high_ref, low_ref):
            ref[:, :, :, :edge] = ref[:, :, :, TILES * LANES:TILES * LANES + edge]
            ref[:, :, :, TILES * LANES + edge:] = ref[:, :, :, edge:2 * edge]
        scale = lax.rsqrt(jnp.sum(square, keepdims=True) / float(SUB ** 3) + 1e-5)
        scale_ref[0] = jnp.broadcast_to(scale, (8, LANES))


def prepare(meta, source):
    slots = meta.shape[1]
    block = (SUB, SUB, LANES)
    spread = pl.BlockSpec((1, 4, SUB, WIDTH), lambda s, m: (s, 0, 0, 0))
    rows = jax.ShapeDtypeStruct((slots, 4, SUB, WIDTH), bf16)
    return pl.pallas_call(
        prepare_kernel,
        out_shape=[rows, rows, jax.ShapeDtypeStruct((slots, 8, LANES), f32)],
        grid_spec=pltpu.PrefetchScalarGridSpec(
            num_scalar_prefetch=1,
            grid=(slots,),
            in_specs=[
                pl.BlockSpec(block, lambda s, m: (0, 0, m[0, s] // LANES)),
                pl.BlockSpec(block, lambda s, m: (0, 0, jnp.minimum(m[0, s] // LANES + 1, 3))),
            ],
            out_specs=[spread, spread, pl.BlockSpec((1, 8, LANES), lambda s, m: (s, 0, 0))],
            scratch_shapes=[pltpu.VMEM((SUB, TILES * LANES), f32)],
        ),
        compiler_params=pltpu.CompilerParams(vmem_limit_bytes=58 * 1024 * 1024),
        cost_estimate=pl.CostEstimate(flops=1, bytes_accessed=1, transcendentals=0),
        name="prepare",
    )(meta, source, source)


def window_copies(parts, refs, meta, slot, buf, window, sem, act):
    own, before_z, after_z, before_y, after_y, corner_before, corner_after = refs
    corner, shift_z, shift_y = meta[1, slot], meta[2, slot], meta[3, slot]
    middle = slice(DMAX, DMAX + SUB)
    edges = slice(0, DMAX), slice(DMAX + SUB, SUB + 2 * DMAX)

    def copy(source, z_rows, y_rows, tile, n):
        act(pltpu.make_async_copy(source, window.at[buf, tile, z_rows, y_rows], sem.at[buf, n, tile]))

    for tile in range(2):
        at = corner // LANES + tile

        @pl.when((tile == 0) | (lax.rem(corner, LANES) > LANES - SUB))
        def _(tile=tile, at=at):
            lanes = tile_at(jnp.minimum(at, 3))
            copy(own.at[:, :, lanes], middle, middle, tile, 0)
            for side, halo in enumerate((before_z, after_z)):
                @pl.when(shift_z < 0 if side == 0 else shift_z > 0)
                def _(side=side, halo=halo):
                    copy(halo.at[:, :, lanes], edges[side], middle, tile, 1)

            for y_side in range(2):
                @pl.when(shift_y < 0 if y_side == 0 else shift_y > 0)
                def _(y_side=y_side):
                    for n, part in enumerate(parts):
                        base = sum(PIECES[:part])

                        @pl.when((at >= base) & (at < base + PIECES[part]))
                        def _(n=n, base=base):
                            here = tile_at(at - base)
                            copy((before_y, after_y)[y_side][n].at[:, :, here], middle, edges[y_side], tile, 2)
                            for z_side in range(2):
                                @pl.when(shift_z < 0 if z_side == 0 else shift_z > 0)
                                def _(z_side=z_side):
                                    piece = (corner_before, corner_after)[z_side][n]
                                    piece = piece.at[:, y_side * DMAX:(y_side + 1) * DMAX, here]
                                    copy(piece, edges[z_side], edges[y_side], tile, 3)


def kernel(call, parts, meta, scales, s_high, s_low, *rest):
    chunks = len(parts)
    own, before_z, after_z = rest[:3]
    pieces = [rest[3 + n * chunks:3 + (n + 1) * chunks] for n in range(4)]
    previous, out, window, flat, s_hi, s_lo, q_hi, q_lo, acc_a, acc_b, order, q_sem, s_sem = rest[3 + 4 * chunks:]
    refs = (own, before_z, after_z, *pieces)
    out[...] = previous[...]

    count, early = jnp.int32(0), jnp.int32(0)
    for slot in range(meta.shape[1]):
        stage = (meta[1, slot] + SUB - 1) // LANES
        live = slot < meta[4, 0]
        first = live & (stage < PIECES[0]) & (early < EARLY)
        early = early + first.astype(jnp.int32)
        mine = (first, live & (stage < 3) & jnp.logical_not(first), live & (stage == 3))[call]

        @pl.when(mine)
        def _(count=count, slot=slot):
            order[count] = slot
        count = count + mine.astype(jnp.int32)

    def windows(n, buf, act):
        window_copies(parts, refs, meta, order[n], buf, window, q_sem, act)

    def sources(n, buf, act):
        act(pltpu.make_async_copy(s_high.at[order[n]], s_hi.at[buf], s_sem.at[buf, 0]))
        act(pltpu.make_async_copy(s_low.at[order[n]], s_lo.at[buf], s_sem.at[buf, 1]))

    start, wait = (lambda copy: copy.start()), (lambda copy: copy.wait())

    def gather(n, buf):
        slot = order[n]
        shift = lax.rem(meta[1, slot], LANES)
        z0, y0 = meta[2, slot] + DMAX, meta[3, slot] + DMAX
        keep = lane_index() >= shift

        def row(z):
            rows = pl.ds(y0, SUB)
            return jnp.where(keep, window[buf, 0, z0 + z, rows, :], window[buf, 1, z0 + z, rows, :])

        def step(i):
            tile = aligned(row, i, shift)
            flat[buf, :, tile_at(i)] = tile
            return fold(tile)

        return step

    def average(total):
        return jnp.sum(total, keepdims=True) / float(SUB ** 3)

    zero = jnp.zeros((8, LANES), f32)
    steps = TILES // CHUNK
    dims = (((1,), (1,)), ((), ()))

    def source_rows(ref, buf, chunk, w):
        rows = []
        for a in range(2):
            for n in range(WIN):
                tz = n - WIN // 2
                parity = tz % 2
                offset = PAD - (tz + parity) // 2
                at = pl.ds(pl.multiple_of((chunk * CHUNK + offset) * LANES, LANES), CHUNK * LANES)
                rows.append(ref[buf, 2 * a + parity, 16 * w:16 * w + 16, at])
        return jnp.concatenate(rows, axis=0)

    def target_rows(ref, side, w):
        rows = []
        for n in range(STEP_X):
            for j in (w, (w + 1) % 4):
                rows.append(ref[side, n * SUB + 16 * j:n * SUB + 16 * j + 16, :])
        return rows

    def multiply(buf, chunk, side):
        lhs = jnp.concatenate([
            jnp.concatenate(target_rows(q_hi, side, w) + target_rows(q_lo, side, w), axis=0) for w in range(4)], axis=1)
        rhs_hi = jnp.concatenate([source_rows(s_hi, buf, chunk, w) for w in range(4)], axis=1)
        rhs_lo = jnp.concatenate([source_rows(s_lo, buf, chunk, w) for w in range(4)], axis=1)
        acc_a[...] += lax.dot_general(lhs, rhs_hi, dims, preferred_element_type=f32)
        acc_b[...] += lax.dot_general(lhs[:128], rhs_lo, dims, preferred_element_type=f32)

    def one_slot(n, buf, mean):
        slot = order[n]

        @pl.when(n + 2 < count)
        def _():
            windows(n + 2, buf, start)

        @pl.when(n + 1 < count)
        def _():
            sources(n + 1, 1 - buf, start)
            windows(n + 1, 1 - buf, wait)

        sources(n, buf, wait)
        gather_step = gather(jnp.minimum(n + 1, count - 1), 1 - buf)

        def build(chunk, side):
            square = zero
            for k in range(CHUNK):
                tile = flat[buf, :, tile_at(chunk * CHUNK + k)] - mean
                square = square + fold(tile * tile)
                tile = jnp.concatenate([tile[56:], tile[:56]], axis=0)
                other = half_roll(tile)
                for b in range(STEP_X):
                    moved = turned(tile, other, b) if b else tile
                    high, low = split(moved)
                    q_hi[side, b * SUB:(b + 1) * SUB, k * LANES:(k + 1) * LANES] = high
                    q_lo[side, b * SUB:(b + 1) * SUB, k * LANES:(k + 1) * LANES] = low
            return square

        acc_a[...] = jnp.zeros_like(acc_a)
        acc_b[...] = jnp.zeros_like(acc_b)
        square = build(0, 0)

        def two_steps(i, carry):
            square, total = carry
            for side in range(2):
                chunk = 2 * i + side
                more = build(lax.rem(chunk + 1, steps), 1 - side)
                square = square + (more if side == 0 else jnp.where(chunk + 1 < steps, more, 0.0))
                multiply(buf, chunk, side)
                for k in range(CHUNK):
                    total = total + gather_step(chunk * CHUNK + k)
            return square, total

        square, total = lax.fori_loop(0, steps // 2, two_steps, (square, zero), unroll=4)
        scale = scales[pl.ds(slot, 1)][0, :1, :1] * lax.rsqrt(average(square) + 1e-5) * (1.0 / float(SUB) ** 1.5)
        sums = (acc_a[:128, :] + acc_a[128:, :] + acc_b[...]).reshape(STEP_X, 32, 256)
        row = lax.broadcasted_iota(jnp.int32, (32, 256), 0)
        column = lax.broadcasted_iota(jnp.int32, (32, 256), 1) % 16
        picked = [jnp.sum(jnp.where((row == column + n + 4)[None], sums, 0.0), axis=1) for n in range(WIN)]
        picked = jnp.concatenate(picked, axis=0)
        group = lax.broadcasted_iota(jnp.int32, (256, LANES), 0) // 16
        chosen = (group == lax.broadcasted_iota(jnp.int32, (256, LANES), 1)).astype(f32)
        result = jnp.dot(picked, chosen, precision=lax.Precision.HIGHEST, preferred_element_type=f32)
        out[pl.ds(slot, 1)] = (result * scale)[None]
        return average(total)

    @pl.when(count > 0)
    def _():
        windows(0, 0, start)
        sources(0, 0, start)

        @pl.when(count > 1)
        def _():
            windows(1, 1, start)

        windows(0, 0, wait)
        first = gather(0, 0)
        total = lax.fori_loop(0, TILES, lambda i, total: total + first(i), zero, unroll=4)

        def two_slots(m, mean):
            mean = one_slot(2 * m, 0, mean)
            return lax.cond(2 * m + 1 < count, lambda: one_slot(2 * m + 1, 1, mean), lambda: mean)

        lax.fori_loop(0, (count + 1) // 2, two_slots, average(total))


def correlate(call, parts, meta, prepared, target, halo_z, halo_y, corners, previous):
    slots = meta.shape[1]
    s_high, s_low, scales = prepared
    pieces = []
    for pair in (halo_y, corners):
        for side in range(2):
            pieces += [pair[n][side] for n in parts]
    any_space = pl.BlockSpec(memory_space=pl.ANY)
    in_vmem = pl.BlockSpec(memory_space=pltpu.VMEM)
    reach = SUB + 2 * DMAX
    return pl.pallas_call(
        functools.partial(kernel, call, parts),
        out_shape=jax.ShapeDtypeStruct((slots, 4 * WIN, LANES), f32),
        in_specs=[pl.BlockSpec(memory_space=pltpu.SMEM), in_vmem] + [any_space] * (5 + len(pieces)) + [in_vmem],
        out_specs=in_vmem,
        scratch_shapes=[
            pltpu.VMEM((2, 2, reach, reach, LANES), f32),
            pltpu.VMEM((2, SUB, TILES * LANES), f32),
            pltpu.VMEM((2, 4, SUB, WIDTH), bf16),
            pltpu.VMEM((2, 4, SUB, WIDTH), bf16),
            pltpu.VMEM((2, STEP_X * SUB, CHUNK * LANES), bf16),
            pltpu.VMEM((2, STEP_X * SUB, CHUNK * LANES), bf16),
            pltpu.VMEM((256, 256), f32),
            pltpu.VMEM((128, 256), f32),
            pltpu.SMEM((slots,), jnp.int32),
            pltpu.SemaphoreType.DMA((2, 4, 2)),
            pltpu.SemaphoreType.DMA((2, 2)),
        ],
        compiler_params=pltpu.CompilerParams(vmem_limit_bytes=58 * 1024 * 1024),
        cost_estimate=pl.CostEstimate(flops=1, bytes_accessed=1, transcendentals=0),
        name="correlate",
    )(meta, scales, s_high, s_low, target, *halo_z, *pieces, previous)


def assemble(out):
    slots = out.shape[0]
    sums = out[:, :, :2 * WIN].reshape(slots, WIN, STEP_X, 2, WIN)
    return sums[:, :, :, ::-1].transpose(0, 4, 1, 3, 2).reshape(slots, WIN ** 3)


def neighbours(axis, low, high):
    peers = lax.axis_size(axis)
    up = [(i, i + 1) for i in range(peers - 1)]
    return lax.ppermute(high, axis, up), lax.ppermute(low, axis, [(j, i) for i, j in up])


def per_device(source_volume, target_volume, live_count, subset_start, patch_start, patch_shift):
    slots = subset_start.shape[-1]
    meta = jnp.stack([
        subset_start[0, 0], patch_start[0, 0], patch_shift[0, 0, 0], patch_shift[0, 0, 1],
        jnp.broadcast_to(live_count[0, 0], (slots,)),
    ])
    cuts, base = [], 0
    for width in PIECES:
        cuts.append(slice(base * LANES, (base + width) * LANES))
        base += width

    def edges(volume, cut):
        return volume[:, :DMAX, cut], volume[:, -DMAX:, cut]

    def send_corners(pair):
        before, after = pair
        low = jnp.concatenate([before[:DMAX], after[:DMAX]], axis=1)
        high = jnp.concatenate([before[-DMAX:], after[-DMAX:]], axis=1)
        return neighbours("gz", low, high)

    low, high, later = lax.optimization_barrier((*edges(target_volume, cuts[0]), target_volume))
    halo_y = [neighbours("gy", low, high)]
    halo_z = neighbours("gz", later[:DMAX], later[-DMAX:])
    prepared = prepare(meta, source_volume)
    halo_y[0], prepared, low, high = lax.optimization_barrier((halo_y[0], prepared, *edges(later, cuts[1])))
    halo_y.append(neighbours("gy", low, high))
    halo_z, before, after = lax.optimization_barrier((halo_z, *halo_y[0]))
    corners = [send_corners((before, after)), send_corners(halo_y[1])]
    out = jnp.zeros((slots, 4 * WIN, LANES), f32)
    out = correlate(0, (0,), meta, prepared, target_volume, halo_z, halo_y, corners, out)
    out = correlate(2, (0, 1), meta, prepared, target_volume, halo_z, halo_y, corners, out)
    return assemble(out)[None, None]


def solution(mesh):
    return jax.shard_map(
        per_device,
        mesh=mesh,
        in_specs=(
            P("gz", "gy", None),
            P("gz", "gy", None),
            P("gz", "gy"),
            P("gz", "gy", None),
            P("gz", "gy", None),
            P("gz", "gy", None, None),
        ),
        out_specs=P("gz", "gy", None, None),
        check_vma=False,
    )
```
